512 devices in a mesh: exp: 64 (over y, x, core), rep: 8 (over z).
Axes of the slice: x: 4, y: 8, z: 8, core: 2. Of those that a mesh axis runs over, the one named last changes fastest.
Arguments:
- tokens: bfloat16 [8192, 8192], P('exp', 'rep'), may hold values from -6 to 6
- down_weight: bfloat16 [8192, 2048], P('rep', 'exp'), may hold values from -0.0625 to 0.0625
- gate_proj: bfloat16 [64, 2048, 2048], P('exp', None, 'rep'), may hold values from -0.125 to 0.125
- up_proj: bfloat16 [64, 2048, 2048], P('exp', None, 'rep'), may hold values from -0.125 to 0.125
- out_proj: bfloat16 [64, 2048, 2048], P('exp', 'rep'), may hold values from -0.125 to 0.125
- up_weight: bfloat16 [2048, 8192], P('exp', 'rep'), may hold values from -0.125 to 0.125
- expert_ids: int32 [8192, 4], P('exp'), may hold values from 0 to 63, all different within a row; in each aligned block of 128 rows (0 to 127, 128 to 255, ...) at most 12 rows name the same one
- route_gates: float32 [8192, 4], P('exp'), may hold values from 0.1 to 1
Outputs:
- mixed: bfloat16 [8192, 8192], P('exp', 'rep')
The draws below stay inside these ranges and needn't reach their ends.
Inputs may be any that keep to these rules, and one draw needn't show every extreme that they name: `expert_ids`: in each aligned block of 128 rows (the tokens of one index of exp), no expert is named by more than 12 rows, a bound that some block reaches.
All inputs are finite; a program needn't handle non-finite values.
Results may differ from the reference program's by a relative error of at most 0.035.
Values may be sent and summed in bfloat16 or wider, within the bound.
No kernel may reach another device: no remote copies, remote signals or barrier semaphores. Data moves between devices by JAX's collectives and lax.ppermute only.
A program may use at most 64 MiB of HBM per device.

```python
import math
import jax
import jax.numpy as jnp
import numpy as np
from jax import lax

D = 8192
L = 2048
H = 2048
TOPK = 4
TOK_DEV = 128
EXPERTS = 64
CAP = 12
TOKENS = 8192
N_REP = 8


def shard_levels(key, dims, split, smallest, top_value):
    def one(dim, shards_of):
        heights = jax.random.uniform(jax.random.fold_in(jax.random.fold_in(key, 6), dim), (shards_of,), jnp.float32, smallest / len(split), top_value / len(split))
        return jnp.repeat(jnp.exp(heights), dims[dim] // shards_of).reshape((-1,) + (1,) * (len(dims) - dim - 1))

    level = one(*split[0])
    for cut in split[1:]:
        level = level * one(*cut)
    return level


def shared_out(key, own, number, rows, count, top, limit, skew):
    order = jax.random.permutation(key, count)
    packed, common = shares(count, rows * top, limit, skew, True), shares(count, rows * top, limit, skew, False)
    places = jnp.arange(count)

    def named(tallies, offset_by):
        used = int((tallies > 0).sum())
        fixed = max(1, used // 4)
        passed = fixed + (places - fixed + offset_by * (used - fixed)) % max(1, count - fixed)
        return jnp.zeros((count,), jnp.int32).at[order[jnp.where(places < fixed, places, passed)]].set(jnp.asarray(tallies, jnp.int32))

    tallies = jnp.where(number % 4 == 0, named(packed, number // 4), named(common, number - number // 4 - 1))
    mixed = jax.random.permutation(jax.random.fold_in(own, 3), count)
    source_of, sink = mixed[0:count // 2 * 2:2], mixed[1:count // 2 * 2:2]
    slack = jnp.minimum(tallies[source_of] - 1, limit - tallies[sink]) // 2
    slack = jnp.where((source_of == order[0]) | (sink == order[0]) | (tallies[sink] == 0), 0, jnp.maximum(slack, 0))
    passed = jax.random.randint(jax.random.fold_in(own, 4), (count // 2,), 0, 1 << 20) % (slack + 1)
    tallies = tallies.at[source_of].add(-passed).at[sink].add(passed)
    members = jnp.searchsorted(jnp.cumsum(tallies), jnp.arange(rows * top), side="right").astype(jnp.int32)
    listing = members.reshape(top, rows).T
    listing = listing[jax.random.permutation(jax.random.fold_in(own, 1), rows)]
    offset_by = jax.random.randint(jax.random.fold_in(own, 2), (rows, 1), 0, top)
    return jnp.take_along_axis(listing, (jnp.arange(top)[None, :] + offset_by) % top, axis=1)


def shares(count, total, reach, lean, full):
    loads = [(1 << 20) // math.isqrt(rank ** lean) + 1 for rank in range(1, count + 1)]
    largest = reach if full else min(reach, max(-(-total // count), total * loads[0] // sum(loads)))
    least = 1 if total - largest >= count - 1 else 0
    holding, rest = [largest] + [least] * (count - 1), total - largest - least * (count - 1)
    while rest > 0:
        movable = [i for i in range(1, count) if holding[i] < largest] or [i for i in range(1, count) if holding[i] < reach]
        pool, left = sum([loads[i] for i in movable]), rest
        for i in movable:
            addition = min(reach - holding[i], max(1, left * loads[i] // pool), rest)
            holding[i] = holding[i] + addition
            rest = rest - addition
    return np.array(holding)


def noise(key, extent, scale, limit, split=(), kind=jnp.bfloat16):
    array = jax.random.normal(key, extent, jnp.float32) * scale
    if len(split) > 0:
        array = shard_levels(key, extent, split, -0.22, 0.18) * array
    return jnp.clip(array, min=-limit, max=limit).astype(kind)


def setup_inputs(seed: int = 0) -> dict:
    arg_keys = jax.random.split(jax.random.key(seed), 9)
    tokens = noise(arg_keys[0], (TOKENS, D), 1.0, 6.0, ((0, 64), (1, 8)))
    down_weight = noise(arg_keys[1], (D, L), D ** -0.5, 0.0625, ((0, 8), (1, 64)))
    gate_proj = noise(arg_keys[2], (EXPERTS, L, H), L ** -0.5, 0.125, ((0, 64), (2, 8)))
    up_proj = noise(arg_keys[3], (EXPERTS, L, H), L ** -0.5, 0.125, ((0, 64), (2, 8)))
    out_proj = noise(arg_keys[4], (EXPERTS, H, L), H ** -0.5, 0.125, ((0, 64), (1, 8)))
    up_weight = noise(arg_keys[5], (L, D), L ** -0.5, 0.125, ((0, 64), (1, 8)))
    expert_ids_keys = jax.random.split(jax.random.fold_in(arg_keys[6], 1), TOKENS // TOK_DEV)
    expert_ids_turns = jax.random.permutation(jax.random.fold_in(arg_keys[6], 3), TOKENS // TOK_DEV)
    expert_ids = jax.vmap(lambda own, number: shared_out(jax.random.fold_in(arg_keys[6], 2), own, number, TOK_DEV, EXPERTS, TOPK, CAP, 2))(expert_ids_keys, expert_ids_turns).reshape((TOKENS, TOPK))
    route_gates = jnp.clip(0.1 + 0.9 * jax.random.uniform(arg_keys[7], (TOKENS, TOPK), jnp.float32) ** shard_levels(arg_keys[7], (TOKENS, TOPK), ((0, 64),), -0.2, 0.2), 0.1, 1.0)
    return {"tokens": tokens, "down_weight": down_weight, "gate_proj": gate_proj, "up_proj": up_proj, "out_proj": out_proj, "up_weight": up_weight, "expert_ids": expert_ids, "route_gates": route_gates}


def slot_targets(flat_ids, capacity):
    position = jnp.arange(flat_ids.shape[0], dtype=jnp.int32)
    same_id = flat_ids[:, None] == flat_ids[None, :]
    earlier = position[:, None] > position[None, :]
    slot_index = jnp.sum((same_id & earlier).astype(jnp.int32), axis=1).astype(jnp.int32)
    return (flat_ids * capacity + slot_index).astype(jnp.int32)


def reference(tokens, down_weight, gate_proj, up_proj, out_proj, up_weight, expert_ids, route_gates):
    latent = jnp.dot(tokens, down_weight, preferred_element_type=jnp.float32).astype(jnp.bfloat16)
    groups = TOKENS // TOK_DEV
    entries = TOK_DEV * TOPK
    flat_ids = expert_ids.reshape(groups, entries).astype(jnp.int32)
    targets = jax.vmap(lambda ids: slot_targets(ids, CAP))(flat_ids)
    owner_row = (jnp.arange(groups, dtype=jnp.int32)[:, None] * TOK_DEV
                 + (jnp.arange(entries, dtype=jnp.int32) // TOPK)[None, :]).astype(jnp.int32)
    source_row = jax.vmap(lambda tg, ow: jnp.zeros((EXPERTS * CAP,), jnp.int32).at[tg].set(ow))(targets, owner_row)
    filled = jax.vmap(lambda tg: jnp.zeros((EXPERTS * CAP,), jnp.bfloat16).at[tg].set(jnp.ones((entries,), jnp.bfloat16)))(targets)
    source_row = source_row.reshape(groups, EXPERTS, CAP)
    filled = filled.reshape(groups, EXPERTS, CAP)
    share = H // N_REP

    def one_expert(index):
        picks = source_row[:, index, :].reshape(-1)
        masks = filled[:, index, :].reshape(-1)
        rows_in = latent[picks] * masks[:, None]
        gate_act = jnp.dot(rows_in, gate_proj[index], preferred_element_type=jnp.float32)
        up_act = jnp.dot(rows_in, up_proj[index], preferred_element_type=jnp.float32)
        hidden = (jax.nn.silu(gate_act) * up_act).astype(jnp.bfloat16)
        split_hidden = hidden.reshape(-1, N_REP, share).astype(jnp.float32)
        split_out = out_proj[index].reshape(N_REP, share, L).astype(jnp.float32)
        terms = jnp.einsum('rnh,nhl->nrl', split_hidden, split_out).astype(jnp.bfloat16)
        terms = lax.optimization_barrier(terms).astype(jnp.float32)
        return jnp.sum(terms, axis=0).reshape(groups, CAP, L)

    expert_out = lax.map(one_expert, jnp.arange(EXPERTS, dtype=jnp.int32))
    slot_of = (targets % CAP).astype(jnp.int32)
    group_of = jnp.broadcast_to(jnp.arange(groups, dtype=jnp.int32)[:, None], (groups, entries))
    picked = expert_out[flat_ids, group_of, slot_of].astype(jnp.float32)
    picked = picked.reshape(TOKENS, TOPK, L)
    combined = jnp.sum(picked * route_gates.astype(jnp.float32)[:, :, None], axis=1).astype(jnp.bfloat16)
    return jnp.dot(combined, up_weight, preferred_element_type=jnp.float32).astype(jnp.bfloat16)
```

```python
import jax
import jax.numpy as jnp
from jax import lax
from jax.sharding import Mesh, PartitionSpec as P


def spread(x, axis):
    copies = jnp.broadcast_to(x[None], (lax.axis_size(axis),) + x.shape)
    return lax.all_to_all(copies, axis, split_axis=0, concat_axis=0, tiled=True)


def expert_counts(ids_t, experts):
    tok = ids_t.shape[1]
    expert = lax.broadcasted_iota(jnp.int32, (experts, tok), 0)
    one_hot = jnp.zeros((experts, tok), jnp.bool_)
    for k in range(ids_t.shape[0]):
        one_hot = one_hot | (ids_t[k][None, :] == expert)
    earlier = lax.broadcasted_iota(jnp.int32, (tok, tok), 0) < lax.broadcasted_iota(
        jnp.int32, (tok, tok), 1
    )
    counts = jnp.dot(
        one_hot.astype(jnp.bfloat16),
        earlier.astype(jnp.bfloat16),
        preferred_element_type=jnp.float32,
    ).astype(jnp.int32)
    return one_hot, counts


def on_device(
    tokens, down_weight, gate_proj, up_proj, out_proj, up_weight, expert_ids, route_gates
):
    tok_rows = tokens.shape[0]
    topk_count = expert_ids.shape[1]
    ny, nk, nr = lax.axis_size("y"), lax.axis_size("k"), lax.axis_size("rep")
    experts = ny * nk
    capacity = max(2, 3 * tok_rows * topk_count // (2 * experts))
    width = gate_proj.shape[1]
    unit = down_weight.shape[1]
    slice_width = width // nr

    swap = [(i * nr + j, j * nr + i) for i in range(nk) for j in range(nr)]
    ids_t = expert_ids.T
    sent_ids_t = lax.ppermute(ids_t, ("k", "rep"), swap)

    all_tokens = lax.all_gather(tokens, "k", axis=0, tiled=True)
    down_cols = spread(down_weight.T, "y").reshape(ny * unit, down_weight.shape[0])
    one_hot, counts = expert_counts(sent_ids_t, experts)
    slot = lax.broadcasted_iota(jnp.int32, (experts, capacity, tok_rows), 1)
    select = ((counts[:, None, :] == slot) & one_hot[:, None, :]).astype(jnp.bfloat16)
    _, own_counts = expert_counts(ids_t, experts)
    own_slot = jnp.take_along_axis(own_counts, ids_t, axis=0)
    targets = (ids_t * capacity + own_slot).T.reshape(-1)

    partial_latent = lax.dot_general(
        all_tokens, down_cols, (((1,), (1,)), ((), ())), preferred_element_type=jnp.float32
    )
    pieces = lax.all_to_all(
        partial_latent.astype(jnp.bfloat16).reshape(nr, tok_rows, ny * unit),
        "rep", split_axis=0, concat_axis=0, tiled=True,
    )
    latent = jnp.sum(pieces.astype(jnp.float32), axis=0).astype(jnp.bfloat16)
    send = lax.dot_general(
        select, latent, (((2,), (0,)), ((), ())), preferred_element_type=jnp.float32
    ).astype(jnp.bfloat16)
    got = lax.all_to_all(send, ("y", "k"), split_axis=0, concat_axis=0, tiled=True)
    rows = got.reshape(ny, nk, capacity, ny * unit).transpose(0, 2, 1, 3)
    rows = rows.reshape(ny * capacity, width)
    rows, up_weight = lax.optimization_barrier((rows, up_weight))
    full_rows = lax.all_gather(rows, "rep", axis=0, tiled=True)
    up_rows = spread(up_weight, "y")

    def reorder(w):
        return w.reshape(ny, nk, unit, w.shape[1]).transpose(1, 0, 2, 3).reshape(w.shape)

    gate_act = jnp.dot(full_rows, reorder(gate_proj[0]), preferred_element_type=jnp.float32)
    up_act = jnp.dot(full_rows, reorder(up_proj[0]), preferred_element_type=jnp.float32)
    hidden = (jax.nn.silu(gate_act) * up_act).astype(jnp.bfloat16)
    partial_out = jnp.dot(
        hidden, out_proj[0], preferred_element_type=jnp.float32
    ).astype(jnp.bfloat16)
    finished = lax.psum_scatter(partial_out, "rep", scatter_dimension=1, tiled=True)
    finished, up_rows = lax.optimization_barrier((finished, up_rows))
    all_up = lax.all_gather(up_rows, "k", axis=0, tiled=False)
    back = finished.reshape(nr, ny, capacity, slice_width).transpose(1, 0, 2, 3)
    returned = lax.all_to_all(
        back.reshape(experts, capacity, slice_width),
        ("y", "k"), split_axis=0, concat_axis=0, tiled=True,
    )
    picked = returned.astype(jnp.float32).reshape(experts * capacity, slice_width)[targets]
    picked = picked.reshape(tok_rows, topk_count, slice_width)
    combined = jnp.sum(picked * route_gates[:, :, None], axis=1).astype(jnp.bfloat16)
    full_latent = spread(combined, "rep").transpose(1, 0, 2).reshape(tok_rows, width)
    all_up = all_up.transpose(1, 0, 2, 3).reshape(width, up_weight.shape[1])
    mixed = jnp.dot(full_latent, all_up, preferred_element_type=jnp.float32)
    return mixed.astype(jnp.bfloat16)


def solution(mesh):
    nexp, nrep = mesh.devices.shape
    fine = Mesh(mesh.devices.reshape(nexp // nrep, nrep, nrep), ("y", "k", "rep"))
    exp = ("y", "k")
    in_specs = (
        P(exp, "rep"),
        P("rep", exp),
        P(exp, None, "rep"),
        P(exp, None, "rep"),
        P(exp, "rep", None),
        P(exp, "rep"),
        P(exp, None),
        P(exp, None),
    )
    return jax.shard_map(
        on_device, mesh=fine, in_specs=in_specs, out_specs=P(exp, "rep"), check_vma=False
    )
```

```python
import functools

import jax
import jax.numpy as jnp
from jax import lax
from jax.experimental import pallas as pl
from jax.experimental.pallas import tpu as pltpu
from jax.sharding import Mesh, PartitionSpec as P


def spread(x, axis):
    copies = jnp.broadcast_to(x[None], (lax.axis_size(axis),) + x.shape)
    return lax.all_to_all(copies, axis, split_axis=0, concat_axis=0, tiled=True)


def expert_counts(ids_t, experts):
    tok = ids_t.shape[1]
    expert = lax.broadcasted_iota(jnp.int32, (experts, tok), 0)
    one_hot = jnp.zeros((experts, tok), jnp.bool_)
    for k in range(ids_t.shape[0]):
        one_hot = one_hot | (ids_t[k][None, :] == expert)
    earlier = lax.broadcasted_iota(jnp.int32, (tok, tok), 0) < lax.broadcasted_iota(
        jnp.int32, (tok, tok), 1
    )
    counts = jnp.dot(
        one_hot.astype(jnp.bfloat16),
        earlier.astype(jnp.bfloat16),
        preferred_element_type=jnp.float32,
    ).astype(jnp.int32)
    return one_hot, counts


def expert_kernel(steps, per, x_ref, gate_ref, up_ref, out_ref, y_ref, gate_sum, up_sum, hidden):
    step = pl.program_id(0)
    depth = x_ref.shape[1] // per

    @pl.when(step == 0)
    def _():
        gate_sum[...] = jnp.zeros_like(gate_sum)
        up_sum[...] = jnp.zeros_like(up_sum)

    @pl.when(step < steps)
    def _():
        for j in range(per):
            x = x_ref[:, j * depth : (j + 1) * depth]
            w = gate_ref[:, j].reshape(depth, gate_ref.shape[3])
            gate_sum[...] += jnp.dot(x, w, preferred_element_type=jnp.float32)
            w = up_ref[:, j].reshape(depth, up_ref.shape[3])
            up_sum[...] += jnp.dot(x, w, preferred_element_type=jnp.float32)

    @pl.when(step == steps - 1)
    def _():
        hidden[...] = (jax.nn.silu(gate_sum[...]) * up_sum[...]).astype(jnp.bfloat16)

    @pl.when(step >= steps)
    def _():
        y_ref[...] = jnp.dot(
            hidden[...], out_ref[...], preferred_element_type=jnp.float32
        ).astype(jnp.bfloat16)


def run_expert(x, gate, up, out, ny, nk, per=2):
    rows, width = x.shape
    hid = gate.shape[1]
    unit = width // (ny * nk)
    steps = nk // per
    cols = width // steps
    first = lambda i: jnp.minimum(i, steps - 1)
    second = lambda i: jnp.maximum(i - steps, 0)
    w_spec = pl.BlockSpec((ny, per, unit, hid), lambda i: (0, first(i), 0, 0))
    return pl.pallas_call(
        functools.partial(expert_kernel, steps, per),
        grid=(2 * steps,),
        in_specs=[
            pl.BlockSpec((rows, cols), lambda i: (0, first(i))),
            w_spec,
            w_spec,
            pl.BlockSpec((hid, cols), lambda i: (0, second(i))),
        ],
        out_specs=pl.BlockSpec((rows, cols), lambda i: (0, second(i))),
        out_shape=jax.ShapeDtypeStruct((rows, width), jnp.bfloat16),
        scratch_shapes=[
            pltpu.VMEM((rows, hid), jnp.float32),
            pltpu.VMEM((rows, hid), jnp.float32),
            pltpu.VMEM((rows, hid), jnp.bfloat16),
        ],
        compiler_params=pltpu.CompilerParams(vmem_limit_bytes=56 * 1024 * 1024),
        cost_estimate=pl.CostEstimate(
            flops=6 * rows * width * hid,
            bytes_accessed=2 * (2 * rows * width + 3 * width * hid),
            transcendentals=rows * hid,
        ),
    )(x, gate.reshape(ny, nk, unit, hid), up.reshape(ny, nk, unit, hid), out)


def mix_kernel(per, x_ref, w_ref, o_ref, total):
    step = pl.program_id(0)

    @pl.when(step == 0)
    def _():
        total[...] = jnp.zeros_like(total)

    for j in range(per):
        w = w_ref[:, j].reshape(x_ref.shape[2], w_ref.shape[3])
        total[...] += jnp.dot(x_ref[j], w, preferred_element_type=jnp.float32)

    @pl.when(step == pl.num_programs(0) - 1)
    def _():
        o_ref[...] = total[...].astype(jnp.bfloat16)


def run_mix(x, w, per=2):
    ny, toks, depth = x.shape
    nk, _, unit, cols = w.shape
    return pl.pallas_call(
        functools.partial(mix_kernel, per),
        grid=(ny // per,),
        in_specs=[
            pl.BlockSpec((per, toks, depth), lambda i: (i, 0, 0)),
            pl.BlockSpec((nk, per, unit, cols), lambda i: (0, i, 0, 0)),
        ],
        out_specs=pl.BlockSpec((toks, cols), lambda i: (0, 0)),
        out_shape=jax.ShapeDtypeStruct((toks, cols), jnp.bfloat16),
        scratch_shapes=[pltpu.VMEM((toks, cols), jnp.float32)],
        compiler_params=pltpu.CompilerParams(vmem_limit_bytes=56 * 1024 * 1024),
        cost_estimate=pl.CostEstimate(
            flops=2 * ny * toks * depth * cols,
            bytes_accessed=2 * ny * depth * cols,
            transcendentals=0,
        ),
    )(x, w)


def on_device(
    tokens, down_weight, gate_proj, up_proj, out_proj, up_weight, expert_ids, route_gates
):
    tok_rows = tokens.shape[0]
    topk_count = expert_ids.shape[1]
    ny, nk, nr = lax.axis_size("y"), lax.axis_size("k"), lax.axis_size("rep")
    experts = ny * nk
    capacity = max(2, 3 * tok_rows * topk_count // (2 * experts))
    width = gate_proj.shape[1]
    unit = down_weight.shape[1]
    slice_width = width // nr

    swap = [(i * nr + j, j * nr + i) for i in range(nk) for j in range(nr)]
    ids_t = expert_ids.T
    sent_ids_t = lax.ppermute(ids_t, ("k", "rep"), swap)

    all_tokens = lax.all_gather(tokens, "k", axis=0, tiled=True)
    down_cols = spread(down_weight.T, "y").reshape(ny * unit, down_weight.shape[0])
    one_hot, counts = expert_counts(sent_ids_t, experts)
    slot = lax.broadcasted_iota(jnp.int32, (experts, capacity, tok_rows), 1)
    select = ((counts[:, None, :] == slot) & one_hot[:, None, :]).astype(jnp.bfloat16)
    _, own_counts = expert_counts(ids_t, experts)
    own_slot = jnp.take_along_axis(own_counts, ids_t, axis=0)
    targets = (ids_t * capacity + own_slot).T.reshape(-1)

    partial_latent = lax.dot_general(
        all_tokens, down_cols, (((1,), (1,)), ((), ())), preferred_element_type=jnp.float32
    )
    partial_latent, select, targets = lax.optimization_barrier(
        (partial_latent.astype(jnp.bfloat16), select, targets)
    )
    pieces = lax.all_to_all(
        partial_latent.reshape(nr, tok_rows, ny * unit),
        "rep", split_axis=0, concat_axis=0, tiled=True,
    )
    latent = jnp.sum(pieces.astype(jnp.float32), axis=0).astype(jnp.bfloat16)
    send = lax.dot_general(
        select, latent, (((2,), (0,)), ((), ())), preferred_element_type=jnp.float32
    ).astype(jnp.bfloat16)
    got = lax.all_to_all(send, ("y", "k"), split_axis=0, concat_axis=0, tiled=True)
    rows = got.reshape(ny, nk, capacity, ny * unit).transpose(0, 2, 1, 3)
    rows = rows.reshape(ny * capacity, width)
    rows, up_weight = lax.optimization_barrier((rows, up_weight))
    full_rows = lax.all_gather(rows, "rep", axis=0, tiled=True)
    up_rows = spread(up_weight, "y")

    partial_out = run_expert(full_rows, gate_proj[0], up_proj[0], out_proj[0], ny, nk)
    finished = lax.psum_scatter(partial_out, "rep", scatter_dimension=1, tiled=True)
    finished, up_rows = lax.optimization_barrier((finished, up_rows))
    all_up = lax.all_gather(up_rows, "k", axis=0, tiled=False)
    back = finished.reshape(nr, ny, capacity, slice_width).transpose(1, 0, 2, 3)
    returned = lax.all_to_all(
        back.reshape(experts, capacity, slice_width),
        ("y", "k"), split_axis=0, concat_axis=0, tiled=True,
    )
    picked = returned.astype(jnp.float32).reshape(experts * capacity, slice_width)[targets]
    picked = picked.reshape(tok_rows, topk_count, slice_width)
    combined = jnp.sum(picked * route_gates[:, :, None], axis=1).astype(jnp.bfloat16)
    return run_mix(spread(combined, "rep"), all_up)


def solution(mesh):
    nexp, nrep = mesh.devices.shape
    fine = Mesh(mesh.devices.reshape(nexp // nrep, nrep, nrep), ("y", "k", "rep"))
    exp = ("y", "k")
    in_specs = (
        P(exp, "rep"),
        P("rep", exp),
        P(exp, None, "rep"),
        P(exp, None, "rep"),
        P(exp, "rep", None),
        P(exp, "rep"),
        P(exp, None),
        P(exp, None),
    )
    return jax.shard_map(
        on_device, mesh=fine, in_specs=in_specs, out_specs=P(exp, "rep"), check_vma=False
    )
```

```python
import functools

import jax
import jax.numpy as jnp
from jax import lax
from jax.experimental import pallas as pl
from jax.experimental.pallas import tpu as pltpu
from jax.sharding import Mesh, PartitionSpec as P


def spread(x, axis):
    copies = jnp.broadcast_to(x[None], (lax.axis_size(axis),) + x.shape)
    return lax.all_to_all(copies, axis, split_axis=0, concat_axis=0, tiled=True)


def expert_counts(ids_t, experts):
    tok = ids_t.shape[1]
    expert = lax.broadcasted_iota(jnp.int32, (experts, tok), 0)
    one_hot = jnp.zeros((experts, tok), jnp.bool_)
    for k in range(ids_t.shape[0]):
        one_hot = one_hot | (ids_t[k][None, :] == expert)
    earlier = lax.broadcasted_iota(jnp.int32, (tok, tok), 0) < lax.broadcasted_iota(
        jnp.int32, (tok, tok), 1
    )
    counts = jnp.dot(
        one_hot.astype(jnp.bfloat16),
        earlier.astype(jnp.bfloat16),
        preferred_element_type=jnp.float32,
    ).astype(jnp.int32)
    return one_hot, counts


def expert_kernel(x_ref, w_ref, out_ref, y_ref):
    hid = out_ref.shape[0]
    act = jnp.dot(x_ref[...], w_ref[...], preferred_element_type=jnp.float32)
    hidden = (jax.nn.silu(act[:, :hid]) * act[:, hid:]).astype(jnp.bfloat16)
    y_ref[...] = jnp.dot(
        hidden, out_ref[...], preferred_element_type=jnp.float32
    ).astype(jnp.bfloat16)


def run_expert(x, w, out, parts=3):
    rows, width = x.shape
    hid = out.shape[0]
    block = rows // parts
    return pl.pallas_call(
        expert_kernel,
        grid=(parts,),
        in_specs=[
            pl.BlockSpec((block, width), lambda i: (i, 0)),
            pl.BlockSpec((width, 2 * hid), lambda i: (0, 0)),
            pl.BlockSpec((hid, width), lambda i: (0, 0)),
        ],
        out_specs=pl.BlockSpec((block, width), lambda i: (i, 0)),
        out_shape=jax.ShapeDtypeStruct((rows, width), jnp.bfloat16),
        compiler_params=pltpu.CompilerParams(vmem_limit_bytes=56 * 1024 * 1024),
        cost_estimate=pl.CostEstimate(
            flops=6 * rows * width * hid,
            bytes_accessed=2 * (2 * rows * width + 3 * width * hid),
            transcendentals=rows * hid,
        ),
    )(x, w, out)


def mix_kernel(per, x_ref, w_ref, o_ref, total):
    step = pl.program_id(0)

    @pl.when(step == 0)
    def _():
        total[...] = jnp.zeros_like(total)

    for j in range(per):
        toks, depth = total.shape[0], 2 * x_ref.shape[2]
        x = jnp.concatenate([x_ref[j, :toks], x_ref[j, toks:]], axis=1)
        w = w_ref[:, j].reshape(depth, w_ref.shape[3])
        total[...] += jnp.dot(x, w, preferred_element_type=jnp.float32)

    @pl.when(step == pl.num_programs(0) - 1)
    def _():
        o_ref[...] = total[...].astype(jnp.bfloat16)


def run_mix(x, w, per=2):
    ny, toks, depth = x.shape[0], x.shape[1] // 2, 2 * x.shape[2]
    nk, _, unit, cols = w.shape
    return pl.pallas_call(
        functools.partial(mix_kernel, per),
        grid=(ny // per,),
        in_specs=[
            pl.BlockSpec((per, 2 * toks, depth // 2), lambda i: (i, 0, 0)),
            pl.BlockSpec((nk, per, unit, cols), lambda i: (0, i, 0, 0)),
        ],
        out_specs=pl.BlockSpec((toks, cols), lambda i: (0, 0)),
        out_shape=jax.ShapeDtypeStruct((toks, cols), jnp.bfloat16),
        scratch_shapes=[pltpu.VMEM((toks, cols), jnp.float32)],
        compiler_params=pltpu.CompilerParams(vmem_limit_bytes=56 * 1024 * 1024),
        cost_estimate=pl.CostEstimate(
            flops=2 * ny * toks * depth * cols,
            bytes_accessed=2 * ny * depth * cols,
            transcendentals=0,
        ),
    )(x, w)


def slot_mask(one_hot, counts, capacity):
    experts, toks = counts.shape
    shape = (experts, 2 * capacity, 2 * toks)
    row = lax.broadcasted_iota(jnp.int32, shape, 1)
    col = lax.broadcasted_iota(jnp.int32, shape, 2)
    row_half = (row >= capacity).astype(jnp.int32)
    col_half = (col >= toks).astype(jnp.int32)
    slot = jnp.where(one_hot, counts, -1)
    slot = jnp.concatenate([slot, slot], axis=1)[:, None, :]
    return (slot == row - capacity * row_half) & (row_half == col_half)


def combine_weights(ids_t, gates_t, experts, capacity):
    one_hot, counts = expert_counts(ids_t, experts)
    expert = lax.broadcasted_iota(jnp.int32, counts.shape, 0)
    gate = jnp.zeros(counts.shape, jnp.float32)
    for k in range(ids_t.shape[0]):
        gate = gate + jnp.where(ids_t[k][None, :] == expert, gates_t[k][None, :], 0.0)
    high = lax.reduce_precision(gate, 8, 7)
    mask = slot_mask(one_hot, counts, capacity)

    def spread_out(g):
        both = jnp.concatenate([g, g], axis=1)[:, None, :]
        return jnp.where(mask, both, 0.0).astype(jnp.bfloat16).reshape(-1, mask.shape[2])

    return spread_out(high), spread_out(gate - high)


def on_device(
    tokens, down_weight, gate_proj, up_proj, out_proj, up_weight, expert_ids, route_gates
):
    tok_rows = tokens.shape[0]
    topk_count = expert_ids.shape[1]
    ny, nk, nr = lax.axis_size("y"), lax.axis_size("k"), lax.axis_size("rep")
    experts = ny * nk
    capacity = max(2, 3 * tok_rows * topk_count // (2 * experts))
    width = gate_proj.shape[1]
    unit = down_weight.shape[1]
    slice_width = width // nr

    swap = [(i * nr + j, j * nr + i) for i in range(nk) for j in range(nr)]
    ids_t = expert_ids.T
    sent_ids_t = lax.ppermute(ids_t, ("k", "rep"), swap)

    all_tokens = lax.all_gather(tokens, "k", axis=0, tiled=True)
    down_cols = spread(down_weight.T, "y").reshape(ny * unit, down_weight.shape[0])
    one_hot, counts = expert_counts(sent_ids_t, experts)
    select = slot_mask(one_hot, counts, capacity).astype(jnp.bfloat16)
    select = select.reshape(2 * experts * capacity, 2 * tok_rows)

    partial_latent = lax.dot_general(
        all_tokens, down_cols, (((1,), (1,)), ((), ())), preferred_element_type=jnp.float32
    )
    partial_latent, select = lax.optimization_barrier(
        (partial_latent.astype(jnp.bfloat16), select)
    )
    pieces = lax.all_to_all(
        partial_latent.reshape(nr, tok_rows, ny * unit),
        "rep", split_axis=0, concat_axis=0, tiled=True,
    )
    latent = jnp.sum(pieces.astype(jnp.float32), axis=0).astype(jnp.bfloat16)
    half = ny * unit // 2
    latent = jnp.concatenate([latent[:, :half], latent[:, half:]], axis=0)
    send = jnp.dot(select, latent, preferred_element_type=jnp.float32).astype(jnp.bfloat16)
    got = lax.all_to_all(
        send.reshape(experts, 2 * capacity, half),
        ("y", "k"), split_axis=0, concat_axis=0, tiled=True,
    )
    rows = got.reshape(ny, nk, 2, capacity, half).transpose(3, 0, 1, 2, 4)
    rows = rows.reshape(capacity * ny, width)
    rows, up_weight = lax.optimization_barrier((rows, up_weight))
    full_rows = lax.all_gather(rows, "rep", axis=0, tiled=True)
    up_rows = spread(up_weight, "y")

    def reorder(w):
        return w.reshape(ny, nk, unit, w.shape[1]).transpose(1, 0, 2, 3).reshape(w.shape)

    high, low = combine_weights(expert_ids.T, route_gates.T, experts, capacity)
    weights = jnp.concatenate([reorder(gate_proj[0]), reorder(up_proj[0])], axis=1)
    full_rows, weights, high, low = lax.optimization_barrier((full_rows, weights, high, low))
    partial_out = run_expert(full_rows, weights, out_proj[0])
    finished = lax.psum_scatter(partial_out, "rep", scatter_dimension=1, tiled=True)
    finished, up_rows = lax.optimization_barrier((finished, up_rows))
    all_up = lax.all_gather(up_rows, "k", axis=0, tiled=False)
    back = finished.reshape(nr, capacity, ny, 2, slice_width // 2).transpose(2, 0, 3, 1, 4)
    returned = lax.all_to_all(
        back.reshape(experts, 2 * capacity, slice_width // 2),
        ("y", "k"), split_axis=0, concat_axis=0, tiled=True,
    )
    returned = returned.reshape(2 * experts * capacity, slice_width // 2)
    combined = sum(
        lax.dot_general(
            g, returned, (((0,), (0,)), ((), ())), preferred_element_type=jnp.float32
        )
        for g in (high, low)
    ).astype(jnp.bfloat16)
    return run_mix(spread(combined, "rep"), all_up)


def solution(mesh):
    nexp, nrep = mesh.devices.shape
    fine = Mesh(mesh.devices.reshape(nexp // nrep, nrep, nrep), ("y", "k", "rep"))
    exp = ("y", "k")
    in_specs = (
        P(exp, "rep"),
        P("rep", exp),
        P(exp, None, "rep"),
        P(exp, None, "rep"),
        P(exp, "rep", None),
        P(exp, "rep"),
        P(exp, None),
        P(exp, None),
    )
    return jax.shard_map(
        on_device, mesh=fine, in_specs=in_specs, out_specs=P(exp, "rep"), check_vma=False
    )
```

```python
import functools

import jax
import jax.numpy as jnp
from jax import lax
from jax.experimental import pallas as pl
from jax.experimental.pallas import tpu as pltpu
from jax.sharding import Mesh, PartitionSpec as P


def spread(x, axis):
    copies = jnp.broadcast_to(x[None], (lax.axis_size(axis),) + x.shape)
    return lax.all_to_all(copies, axis, split_axis=0, concat_axis=0, tiled=True)


def expert_counts(ids_t, experts):
    tok = ids_t.shape[1]
    expert = lax.broadcasted_iota(jnp.int32, (experts, tok), 0)
    one_hot = jnp.zeros((experts, tok), jnp.bool_)
    for k in range(ids_t.shape[0]):
        one_hot = one_hot | (ids_t[k][None, :] == expert)
    earlier = lax.broadcasted_iota(jnp.int32, (tok, tok), 0) < lax.broadcasted_iota(
        jnp.int32, (tok, tok), 1
    )
    counts = jnp.dot(
        one_hot.astype(jnp.bfloat16),
        earlier.astype(jnp.bfloat16),
        preferred_element_type=jnp.float32,
    ).astype(jnp.int32)
    return one_hot, counts


def expert_kernel(x_ref, w_ref, out_ref, y_ref):
    hid = out_ref.shape[0]
    act = jnp.dot(x_ref[...], w_ref[...], preferred_element_type=jnp.float32)
    hidden = (jax.nn.silu(act[:, :hid]) * act[:, hid:]).astype(jnp.bfloat16)
    chunk = min(512, y_ref.shape[1])
    for c in range(0, y_ref.shape[1], chunk):
        y_ref[:, c : c + chunk] = jnp.dot(
            hidden, out_ref[:, c : c + chunk], preferred_element_type=jnp.float32
        ).astype(jnp.bfloat16)


def run_expert(x, w, out, parts=2):
    rows, width = x.shape
    hid = out.shape[0]
    block = rows // parts
    return pl.pallas_call(
        expert_kernel,
        grid=(parts,),
        in_specs=[
            pl.BlockSpec((block, width), lambda i: (i, 0)),
            pl.BlockSpec((width, 2 * hid), lambda i: (0, 0)),
            pl.BlockSpec((hid, width), lambda i: (0, 0)),
        ],
        out_specs=pl.BlockSpec((block, width), lambda i: (i, 0)),
        out_shape=jax.ShapeDtypeStruct((rows, width), jnp.bfloat16),
        compiler_params=pltpu.CompilerParams(vmem_limit_bytes=56 * 1024 * 1024),
        cost_estimate=pl.CostEstimate(
            flops=6 * rows * width * hid,
            bytes_accessed=2 * (2 * rows * width + 3 * width * hid),
            transcendentals=rows * hid,
        ),
    )(x, w, out)


def mix_kernel(per, x_ref, w_ref, o_ref, total):
    step = pl.program_id(0)

    @pl.when(step == 0)
    def _():
        total[...] = jnp.zeros_like(total)

    for j in range(per):
        toks, depth = total.shape[0], 2 * x_ref.shape[2]
        x = jnp.concatenate([x_ref[j, :toks], x_ref[j, toks:]], axis=1)
        w = w_ref[:, j].reshape(depth, w_ref.shape[3])
        total[...] += jnp.dot(x, w, preferred_element_type=jnp.float32)

    @pl.when(step == pl.num_programs(0) - 1)
    def _():
        o_ref[...] = total[...].astype(jnp.bfloat16)


def run_mix(x, w, per=4):
    ny, toks, depth = x.shape[0], x.shape[1] // 2, 2 * x.shape[2]
    nk, _, unit, cols = w.shape
    return pl.pallas_call(
        functools.partial(mix_kernel, per),
        grid=(ny // per,),
        in_specs=[
            pl.BlockSpec((per, 2 * toks, depth // 2), lambda i: (i, 0, 0)),
            pl.BlockSpec((nk, per, unit, cols), lambda i: (0, i, 0, 0)),
        ],
        out_specs=pl.BlockSpec((toks, cols), lambda i: (0, 0)),
        out_shape=jax.ShapeDtypeStruct((toks, cols), jnp.bfloat16),
        scratch_shapes=[pltpu.VMEM((toks, cols), jnp.float32)],
        compiler_params=pltpu.CompilerParams(vmem_limit_bytes=56 * 1024 * 1024),
        cost_estimate=pl.CostEstimate(
            flops=2 * ny * toks * depth * cols,
            bytes_accessed=2 * ny * depth * cols,
            transcendentals=0,
        ),
    )(x, w)


def slot_mask(one_hot, counts, capacity):
    experts, toks = counts.shape
    shape = (experts, 2 * capacity, 2 * toks)
    row = lax.broadcasted_iota(jnp.int32, shape, 1)
    col = lax.broadcasted_iota(jnp.int32, shape, 2)
    row_half = (row >= capacity).astype(jnp.int32)
    col_half = (col >= toks).astype(jnp.int32)
    slot = jnp.where(one_hot, counts, -1)
    slot = jnp.concatenate([slot, slot], axis=1)[:, None, :]
    return (slot == row - capacity * row_half) & (row_half == col_half)


def combine_weights(ids_t, gates_t, experts, capacity):
    one_hot, counts = expert_counts(ids_t, experts)
    expert = lax.broadcasted_iota(jnp.int32, counts.shape, 0)
    gate = jnp.zeros(counts.shape, jnp.float32)
    for k in range(ids_t.shape[0]):
        gate = gate + jnp.where(ids_t[k][None, :] == expert, gates_t[k][None, :], 0.0)
    high = lax.reduce_precision(gate, 8, 7)
    mask = slot_mask(one_hot, counts, capacity)

    def spread_out(g):
        both = jnp.concatenate([g, g], axis=1)[:, None, :]
        return jnp.where(mask, both, 0.0).astype(jnp.bfloat16).reshape(-1, mask.shape[2])

    return spread_out(high), spread_out(gate - high)


def on_device(
    tokens, down_weight, gate_proj, up_proj, out_proj, up_weight, expert_ids, route_gates
):
    tok_rows = tokens.shape[0]
    topk_count = expert_ids.shape[1]
    ny, nk, nr = lax.axis_size("y"), lax.axis_size("k"), lax.axis_size("rep")
    experts = ny * nk
    capacity = max(2, 3 * tok_rows * topk_count // (2 * experts))
    width = gate_proj.shape[1]
    unit = down_weight.shape[1]
    slice_width = width // nr

    all_tokens = lax.all_gather(tokens, "k", axis=0, tiled=True)
    down_cols = spread(down_weight.T, "y").reshape(ny * unit, down_weight.shape[0])
    swap = [(i * nr + j, j * nr + i) for i in range(nk) for j in range(nr)]
    ids_t, _ = lax.optimization_barrier((expert_ids.T, down_cols))
    sent_ids_t = lax.ppermute(ids_t, ("k", "rep"), swap)
    one_hot, counts = expert_counts(sent_ids_t, experts)
    select = slot_mask(one_hot, counts, capacity).astype(jnp.bfloat16)
    select = select.reshape(2 * experts * capacity, 2 * tok_rows)

    partial_latent = lax.dot_general(
        all_tokens, down_cols, (((1,), (1,)), ((), ())), preferred_element_type=jnp.float32
    )
    pieces = lax.all_to_all(
        partial_latent.astype(jnp.bfloat16).reshape(nr, tok_rows, ny * unit),
        "rep", split_axis=0, concat_axis=0, tiled=True,
    )
    latent = jnp.sum(pieces.astype(jnp.float32), axis=0).astype(jnp.bfloat16)
    half = ny * unit // 2
    latent = jnp.concatenate([latent[:, :half], latent[:, half:]], axis=0)
    send = jnp.dot(select, latent, preferred_element_type=jnp.float32).astype(jnp.bfloat16)
    got = lax.all_to_all(
        send.reshape(experts, 2 * capacity, half),
        ("y", "k"), split_axis=0, concat_axis=0, tiled=True,
    )
    rows = got.reshape(ny, nk, 2, capacity, half).transpose(3, 0, 1, 2, 4)
    rows = rows.reshape(capacity * ny, width)
    rows, up_weight = lax.optimization_barrier((rows, up_weight))
    full_rows = lax.all_gather(rows, "rep", axis=0, tiled=True)
    up_rows = spread(up_weight, "y")

    def reorder(w):
        return w.reshape(ny, nk, unit, w.shape[1]).transpose(1, 0, 2, 3).reshape(w.shape)

    high, low = combine_weights(expert_ids.T, route_gates.T, experts, capacity)
    weights = jnp.concatenate([reorder(gate_proj[0]), reorder(up_proj[0])], axis=1)
    full_rows, weights, high, low = lax.optimization_barrier((full_rows, weights, high, low))
    partial_out = run_expert(full_rows, weights, out_proj[0])
    finished = lax.psum_scatter(partial_out, "rep", scatter_dimension=1, tiled=True)
    finished, up_rows = lax.optimization_barrier((finished, up_rows))
    all_up = lax.all_gather(up_rows, "k", axis=0, tiled=False)
    back = finished.reshape(nr, capacity, ny, 2, slice_width // 2).transpose(2, 0, 3, 1, 4)
    returned = lax.all_to_all(
        back.reshape(experts, 2 * capacity, slice_width // 2),
        ("y", "k"), split_axis=0, concat_axis=0, tiled=True,
    )
    returned = returned.reshape(2 * experts * capacity, slice_width // 2)
    combined = sum(
        lax.dot_general(
            g, returned, (((0,), (0,)), ((), ())), preferred_element_type=jnp.float32
        )
        for g in (high, low)
    ).astype(jnp.bfloat16)
    return run_mix(spread(combined, "rep"), all_up)


def solution(mesh):
    nexp, nrep = mesh.devices.shape
    fine = Mesh(mesh.devices.reshape(nexp // nrep, nrep, nrep), ("y", "k", "rep"))
    exp = ("y", "k")
    in_specs = (
        P(exp, "rep"),
        P("rep", exp),
        P(exp, None, "rep"),
        P(exp, None, "rep"),
        P(exp, "rep", None),
        P(exp, "rep"),
        P(exp, None),
        P(exp, None),
    )
    return jax.shard_map(
        on_device, mesh=fine, in_specs=in_specs, out_specs=P(exp, "rep"), check_vma=False
    )
```

```python
import functools

import jax
import jax.numpy as jnp
from jax import lax
from jax.experimental import pallas as pl
from jax.experimental.pallas import tpu as pltpu
from jax.sharding import Mesh, PartitionSpec as P


def spread(x, axis):
    copies = jnp.broadcast_to(x[None], (lax.axis_size(axis),) + x.shape)
    return lax.all_to_all(copies, axis, split_axis=0, concat_axis=0, tiled=True)


def expert_counts(ids_t, experts):
    tok = ids_t.shape[1]
    expert = lax.broadcasted_iota(jnp.int32, (experts, tok), 0)
    one_hot = jnp.zeros((experts, tok), jnp.bool_)
    for k in range(ids_t.shape[0]):
        one_hot = one_hot | (ids_t[k][None, :] == expert)
    earlier = lax.broadcasted_iota(jnp.int32, (tok, tok), 0) < lax.broadcasted_iota(
        jnp.int32, (tok, tok), 1
    )
    counts = jnp.dot(
        one_hot.astype(jnp.bfloat16),
        earlier.astype(jnp.bfloat16),
        preferred_element_type=jnp.float32,
    ).astype(jnp.int32)
    return one_hot, counts


def expert_kernel(x_ref, w_ref, out_ref, y_ref):
    hid = out_ref.shape[0]
    act = jnp.dot(x_ref[...], w_ref[...], preferred_element_type=jnp.float32)
    hidden = (jax.nn.silu(act[:, :hid]) * act[:, hid:]).astype(jnp.bfloat16)
    pieces = y_ref.shape[0] if len(y_ref.shape) == 3 else 4
    chunk = out_ref.shape[1] // pieces
    for c in range(pieces):
        y = jnp.dot(
            hidden, out_ref[:, c * chunk : (c + 1) * chunk], preferred_element_type=jnp.float32
        ).astype(jnp.bfloat16)
        if len(y_ref.shape) == 3:
            y_ref[c] = y
        else:
            y_ref[:, c * chunk : (c + 1) * chunk] = y


def run_expert(x, w, out, block, first, parts, pieces=None):
    width = x.shape[1]
    hid = out.shape[0]
    rows = block * parts
    if pieces is None:
        out_spec = pl.BlockSpec((block, width), lambda i: (i, 0))
        shape = (rows, width)
    else:
        out_spec = pl.BlockSpec((pieces, block, width // pieces), lambda i: (0, i, 0))
        shape = (pieces, rows, width // pieces)
    return pl.pallas_call(
        expert_kernel,
        grid=(parts,),
        in_specs=[
            pl.BlockSpec((block, width), lambda i: (i + first, 0)),
            pl.BlockSpec((width, 2 * hid), lambda i: (0, 0)),
            pl.BlockSpec((hid, width), lambda i: (0, 0)),
        ],
        out_specs=out_spec,
        out_shape=jax.ShapeDtypeStruct(shape, jnp.bfloat16),
        compiler_params=pltpu.CompilerParams(vmem_limit_bytes=56 * 1024 * 1024),
        cost_estimate=pl.CostEstimate(
            flops=6 * rows * width * hid,
            bytes_accessed=2 * (2 * rows * width + 3 * width * hid),
            transcendentals=rows * hid,
        ),
    )(x, w, out)


def mix_kernel(per, x_ref, w_ref, o_ref, total):
    step = pl.program_id(0)

    @pl.when(step == 0)
    def _():
        total[...] = jnp.zeros_like(total)

    for j in range(per):
        toks, depth = total.shape[0], 2 * x_ref.shape[2]
        x = jnp.concatenate([x_ref[j, :toks], x_ref[j, toks:]], axis=1)
        w = w_ref[:, j].reshape(depth, w_ref.shape[3])
        total[...] += jnp.dot(x, w, preferred_element_type=jnp.float32)

    @pl.when(step == pl.num_programs(0) - 1)
    def _():
        o_ref[...] = total[...].astype(jnp.bfloat16)


def run_mix(x, w, per=4):
    ny, toks, depth = x.shape[0], x.shape[1] // 2, 2 * x.shape[2]
    nk, _, unit, cols = w.shape
    return pl.pallas_call(
        functools.partial(mix_kernel, per),
        grid=(ny // per,),
        in_specs=[
            pl.BlockSpec((per, 2 * toks, depth // 2), lambda i: (i, 0, 0)),
            pl.BlockSpec((nk, per, unit, cols), lambda i: (0, i, 0, 0)),
        ],
        out_specs=pl.BlockSpec((toks, cols), lambda i: (0, 0)),
        out_shape=jax.ShapeDtypeStruct((toks, cols), jnp.bfloat16),
        scratch_shapes=[pltpu.VMEM((toks, cols), jnp.float32)],
        compiler_params=pltpu.CompilerParams(vmem_limit_bytes=56 * 1024 * 1024),
        cost_estimate=pl.CostEstimate(
            flops=2 * ny * toks * depth * cols,
            bytes_accessed=2 * ny * depth * cols,
            transcendentals=0,
        ),
    )(x, w)


def slot_mask(one_hot, counts, capacity):
    experts, toks = counts.shape
    shape = (experts, 2 * capacity, 2 * toks)
    row = lax.broadcasted_iota(jnp.int32, shape, 1)
    col = lax.broadcasted_iota(jnp.int32, shape, 2)
    row_half = (row >= capacity).astype(jnp.int32)
    col_half = (col >= toks).astype(jnp.int32)
    slot = jnp.where(one_hot, counts, -1)
    slot = jnp.concatenate([slot, slot], axis=1)[:, None, :]
    return (slot == row - capacity * row_half) & (row_half == col_half)


def combine_weights(ids_t, gates_t, experts, capacity):
    one_hot, counts = expert_counts(ids_t, experts)
    expert = lax.broadcasted_iota(jnp.int32, counts.shape, 0)
    gate = jnp.zeros(counts.shape, jnp.float32)
    for k in range(ids_t.shape[0]):
        gate = gate + jnp.where(ids_t[k][None, :] == expert, gates_t[k][None, :], 0.0)
    high = lax.reduce_precision(gate, 8, 7)
    mask = slot_mask(one_hot, counts, capacity)

    def spread_out(g):
        both = jnp.concatenate([g, g], axis=1)[:, None, :]
        return jnp.where(mask, both, 0.0).astype(jnp.bfloat16).reshape(-1, mask.shape[2])

    return spread_out(high), spread_out(gate - high)


def on_device(
    tokens, down_weight, gate_proj, up_proj, out_proj, up_weight, expert_ids, route_gates
):
    tok_rows = tokens.shape[0]
    topk_count = expert_ids.shape[1]
    ny, nk, nr = lax.axis_size("y"), lax.axis_size("k"), lax.axis_size("rep")
    experts = ny * nk
    capacity = max(2, 3 * tok_rows * topk_count // (2 * experts))
    width = gate_proj.shape[1]
    unit = down_weight.shape[1]
    slice_width = width // nr

    swap = [(i * nr + j, j * nr + i) for i in range(nk) for j in range(nr)]
    ids_t = expert_ids.T
    sent_ids_t = lax.ppermute(ids_t, ("k", "rep"), swap)

    all_tokens = lax.all_gather(tokens, "k", axis=0, tiled=True)
    down_cols = spread(down_weight.T, "y").reshape(ny * unit, down_weight.shape[0])
    one_hot, counts = expert_counts(sent_ids_t, experts)
    select = slot_mask(one_hot, counts, capacity).astype(jnp.bfloat16)
    select = select.reshape(2 * experts * capacity, 2 * tok_rows)

    partial_latent = lax.dot_general(
        all_tokens, down_cols, (((1,), (1,)), ((), ())), preferred_element_type=jnp.float32
    )
    partial_latent, select = lax.optimization_barrier(
        (partial_latent.astype(jnp.bfloat16), select)
    )
    pieces = lax.all_to_all(
        partial_latent.reshape(nr, tok_rows, ny * unit),
        "rep", split_axis=0, concat_axis=0, tiled=True,
    )
    latent = jnp.sum(pieces.astype(jnp.float32), axis=0).astype(jnp.bfloat16)
    half = ny * unit // 2
    latent = jnp.concatenate([latent[:, :half], latent[:, half:]], axis=0)
    send = jnp.dot(select, latent, preferred_element_type=jnp.float32).astype(jnp.bfloat16)
    got = lax.all_to_all(
        send.reshape(experts, 2 * capacity, half),
        ("y", "k"), split_axis=0, concat_axis=0, tiled=True,
    )
    rows = got.reshape(ny, nk, 2, capacity, half).transpose(3, 0, 1, 2, 4)
    rows = rows.reshape(capacity * ny, width)
    rows, up_weight = lax.optimization_barrier((rows, up_weight))
    full_rows = lax.all_gather(rows, "rep", axis=0, tiled=True)
    up_rows = spread(up_weight, "y")

    def reorder(w):
        return w.reshape(ny, nk, unit, w.shape[1]).transpose(1, 0, 2, 3).reshape(w.shape)

    high, low = combine_weights(expert_ids.T, route_gates.T, experts, capacity)
    weights = jnp.concatenate([reorder(gate_proj[0]), reorder(up_proj[0])], axis=1)
    full_rows, weights, high, low, up_rows = lax.optimization_barrier(
        (full_rows, weights, high, low, up_rows)
    )
    per_source = capacity * ny
    late = 3 * nr // 8
    early_rows = (nr - late) * per_source
    early_out = run_expert(full_rows, weights, out_proj[0], early_rows // 2, 0, 2)
    late_in, early_out = lax.optimization_barrier((full_rows, early_out))
    late_out = run_expert(
        late_in, weights, out_proj[0], per_source, nr - late, late, pieces=nr
    )
    finished = lax.psum_scatter(early_out, "rep", scatter_dimension=1, tiled=True)
    late_terms = lax.all_to_all(late_out, "rep", split_axis=0, concat_axis=0, tiled=True)
    late_sum = jnp.sum(late_terms.astype(jnp.float32), axis=0).astype(jnp.bfloat16)
    finished, up_rows, late_sum = lax.optimization_barrier((finished, up_rows, late_sum))
    all_up = lax.all_gather(up_rows, "k", axis=0, tiled=False)
    finished = jnp.concatenate([finished, late_sum], axis=0)
    back = finished.reshape(nr, capacity, ny, 2, slice_width // 2).transpose(2, 0, 3, 1, 4)
    returned = lax.all_to_all(
        back.reshape(experts, 2 * capacity, slice_width // 2),
        ("y", "k"), split_axis=0, concat_axis=0, tiled=True,
    )
    returned = returned.reshape(2 * experts * capacity, slice_width // 2)
    combined = sum(
        lax.dot_general(
            g, returned, (((0,), (0,)), ((), ())), preferred_element_type=jnp.float32
        )
        for g in (high, low)
    ).astype(jnp.bfloat16)
    return run_mix(spread(combined, "rep"), all_up)


def solution(mesh):
    nexp, nrep = mesh.devices.shape
    fine = Mesh(mesh.devices.reshape(nexp // nrep, nrep, nrep), ("y", "k", "rep"))
    exp = ("y", "k")
    in_specs = (
        P(exp, "rep"),
        P("rep", exp),
        P(exp, None, "rep"),
        P(exp, None, "rep"),
        P(exp, "rep", None),
        P(exp, "rep"),
        P(exp, None),
        P(exp, None),
    )
    return jax.shard_map(
        on_device, mesh=fine, in_specs=in_specs, out_specs=P(exp, "rep"), check_vma=False
    )
```

```python
import functools

import jax
import jax.numpy as jnp
from jax import lax
from jax.experimental import pallas as pl
from jax.experimental.pallas import tpu as pltpu
from jax.sharding import Mesh, PartitionSpec as P


def spread(x, axis):
    copies = jnp.broadcast_to(x[None], (lax.axis_size(axis),) + x.shape)
    return lax.all_to_all(copies, axis, split_axis=0, concat_axis=0, tiled=True)


def expert_counts(ids_t, experts):
    tok = ids_t.shape[1]
    expert = lax.broadcasted_iota(jnp.int32, (experts, tok), 0)
    one_hot = jnp.zeros((experts, tok), jnp.bool_)
    for k in range(ids_t.shape[0]):
        one_hot = one_hot | (ids_t[k][None, :] == expert)
    earlier = lax.broadcasted_iota(jnp.int32, (tok, tok), 0) < lax.broadcasted_iota(
        jnp.int32, (tok, tok), 1
    )
    counts = jnp.dot(
        one_hot.astype(jnp.bfloat16),
        earlier.astype(jnp.bfloat16),
        preferred_element_type=jnp.float32,
    ).astype(jnp.int32)
    return one_hot, counts


def expert_kernel(x_ref, w_ref, out_ref, y_ref):
    hid = out_ref.shape[0]
    act = jnp.dot(x_ref[...], w_ref[...], preferred_element_type=jnp.float32)
    hidden = (jax.nn.silu(act[:, :hid]) * act[:, hid:]).astype(jnp.bfloat16)
    chunk = min(512, y_ref.shape[1])
    for c in range(0, y_ref.shape[1], chunk):
        y_ref[:, c : c + chunk] = jnp.dot(
            hidden, out_ref[:, c : c + chunk], preferred_element_type=jnp.float32
        ).astype(jnp.bfloat16)


def run_expert(x, w, out, parts=2):
    rows, width = x.shape
    hid = out.shape[0]
    block = rows // parts
    return pl.pallas_call(
        expert_kernel,
        grid=(parts,),
        in_specs=[
            pl.BlockSpec((block, width), lambda i: (i, 0)),
            pl.BlockSpec((width, 2 * hid), lambda i: (0, 0)),
            pl.BlockSpec((hid, width), lambda i: (0, 0)),
        ],
        out_specs=pl.BlockSpec((block, width), lambda i: (i, 0)),
        out_shape=jax.ShapeDtypeStruct((rows, width), jnp.bfloat16),
        compiler_params=pltpu.CompilerParams(vmem_limit_bytes=56 * 1024 * 1024),
        cost_estimate=pl.CostEstimate(
            flops=6 * rows * width * hid,
            bytes_accessed=2 * (2 * rows * width + 3 * width * hid),
            transcendentals=rows * hid,
        ),
    )(x, w, out)


def mix_kernel(per, x_ref, w_ref, o_ref, total):
    step = pl.program_id(0)

    @pl.when(step == 0)
    def _():
        total[...] = jnp.zeros_like(total)

    for j in range(per):
        toks, depth = total.shape[0], 2 * x_ref.shape[2]
        x = jnp.concatenate([x_ref[j, :toks], x_ref[j, toks:]], axis=1)
        w = w_ref[:, j].reshape(depth, w_ref.shape[3])
        total[...] += jnp.dot(x, w, preferred_element_type=jnp.float32)

    @pl.when(step == pl.num_programs(0) - 1)
    def _():
        o_ref[...] = total[...].astype(jnp.bfloat16)


def run_mix(x, w, per=4):
    ny, toks, depth = x.shape[0], x.shape[1] // 2, 2 * x.shape[2]
    nk, _, unit, cols = w.shape
    return pl.pallas_call(
        functools.partial(mix_kernel, per),
        grid=(ny // per,),
        in_specs=[
            pl.BlockSpec((per, 2 * toks, depth // 2), lambda i: (i, 0, 0)),
            pl.BlockSpec((nk, per, unit, cols), lambda i: (0, i, 0, 0)),
        ],
        out_specs=pl.BlockSpec((toks, cols), lambda i: (0, 0)),
        out_shape=jax.ShapeDtypeStruct((toks, cols), jnp.bfloat16),
        scratch_shapes=[pltpu.VMEM((toks, cols), jnp.float32)],
        compiler_params=pltpu.CompilerParams(vmem_limit_bytes=56 * 1024 * 1024),
        cost_estimate=pl.CostEstimate(
            flops=2 * ny * toks * depth * cols,
            bytes_accessed=2 * ny * depth * cols,
            transcendentals=0,
        ),
    )(x, w)


def slot_mask(one_hot, counts, capacity):
    experts, toks = counts.shape
    shape = (experts, 2 * capacity, 2 * toks)
    row = lax.broadcasted_iota(jnp.int32, shape, 1)
    col = lax.broadcasted_iota(jnp.int32, shape, 2)
    row_half = (row >= capacity).astype(jnp.int32)
    col_half = (col >= toks).astype(jnp.int32)
    slot = jnp.where(one_hot, counts, -1)
    slot = jnp.concatenate([slot, slot], axis=1)[:, None, :]
    return (slot == row - capacity * row_half) & (row_half == col_half)


def combine_weights(ids_t, gates_t, experts, capacity):
    one_hot, counts = expert_counts(ids_t, experts)
    expert = lax.broadcasted_iota(jnp.int32, counts.shape, 0)
    gate = jnp.zeros(counts.shape, jnp.float32)
    for k in range(ids_t.shape[0]):
        gate = gate + jnp.where(ids_t[k][None, :] == expert, gates_t[k][None, :], 0.0)
    high = lax.reduce_precision(gate, 8, 7)
    mask = slot_mask(one_hot, counts, capacity)

    def spread_out(g):
        both = jnp.concatenate([g, g], axis=1)[:, None, :]
        return jnp.where(mask, both, 0.0).astype(jnp.bfloat16).reshape(-1, mask.shape[2])

    return spread_out(high), spread_out(gate - high)


def on_device(
    tokens, down_weight, gate_proj, up_proj, out_proj, up_weight, expert_ids, route_gates
):
    tok_rows = tokens.shape[0]
    topk_count = expert_ids.shape[1]
    ny, nk, nr = lax.axis_size("y"), lax.axis_size("k"), lax.axis_size("rep")
    experts = ny * nk
    capacity = max(2, 3 * tok_rows * topk_count // (2 * experts))
    width = gate_proj.shape[1]
    unit = down_weight.shape[1]
    slice_width = width // nr

    swap = [(i * nr + j, j * nr + i) for i in range(nk) for j in range(nr)]
    ids_t = expert_ids.T
    sent_ids_t = lax.ppermute(ids_t, ("k", "rep"), swap)

    all_tokens = lax.all_gather(tokens, "k", axis=0, tiled=True)
    down_cols = spread(down_weight.T, "y").reshape(ny * unit, down_weight.shape[0])
    one_hot, counts = expert_counts(sent_ids_t, experts)
    select = slot_mask(one_hot, counts, capacity).astype(jnp.bfloat16)
    select = select.reshape(2 * experts * capacity, 2 * tok_rows)

    partial_latent = lax.dot_general(
        all_tokens, down_cols, (((1,), (1,)), ((), ())), preferred_element_type=jnp.float32
    )
    partial_latent, select = lax.optimization_barrier(
        (partial_latent.astype(jnp.bfloat16), select)
    )
    pieces = lax.all_to_all(
        partial_latent.reshape(nr, tok_rows, ny * unit),
        "rep", split_axis=0, concat_axis=0, tiled=True,
    )
    latent = jnp.sum(pieces.astype(jnp.float32), axis=0).astype(jnp.bfloat16)
    half = ny * unit // 2
    latent = jnp.concatenate([latent[:, :half], latent[:, half:]], axis=0)
    send = jnp.dot(select, latent, preferred_element_type=jnp.float32).astype(jnp.bfloat16)
    got = lax.all_to_all(
        send.reshape(experts, 2 * capacity, half),
        ("y", "k"), split_axis=0, concat_axis=0, tiled=True,
    )
    rows = got.reshape(ny, nk, 2, capacity, half).transpose(3, 0, 1, 2, 4)
    rows = rows.reshape(capacity * ny, width)
    rows, up_weight = lax.optimization_barrier((rows, up_weight))
    full_rows = lax.all_gather(rows, "rep", axis=0, tiled=True)
    up_rows = spread(up_weight, "y")

    def reorder(w):
        return w.reshape(ny, nk, unit, w.shape[1]).transpose(1, 0, 2, 3).reshape(w.shape)

    high, low = combine_weights(expert_ids.T, route_gates.T, experts, capacity)
    weights = jnp.concatenate([reorder(gate_proj[0]), reorder(up_proj[0])], axis=1)
    full_rows, weights, high, low, up_rows = lax.optimization_barrier(
        (full_rows, weights, high, low, up_rows)
    )
    partial_out = run_expert(full_rows, weights, out_proj[0])
    finished = lax.psum_scatter(partial_out, "rep", scatter_dimension=1, tiled=True)
    finished, up_rows = lax.optimization_barrier((finished, up_rows))
    all_up = lax.all_gather(up_rows, "k", axis=0, tiled=False)
    back = finished.reshape(nr, capacity, ny, 2, slice_width // 2).transpose(2, 0, 3, 1, 4)
    returned = lax.all_to_all(
        back.reshape(experts, 2 * capacity, slice_width // 2),
        ("y", "k"), split_axis=0, concat_axis=0, tiled=True,
    )
    returned = returned.reshape(2 * experts * capacity, slice_width // 2)
    combined = sum(
        lax.dot_general(
            g, returned, (((0,), (0,)), ((), ())), preferred_element_type=jnp.float32
        )
        for g in (high, low)
    ).astype(jnp.bfloat16)
    return run_mix(spread(combined, "rep"), all_up)


def solution(mesh):
    nexp, nrep = mesh.devices.shape
    fine = Mesh(mesh.devices.reshape(nexp // nrep, nrep, nrep), ("y", "k", "rep"))
    exp = ("y", "k")
    in_specs = (
        P(exp, "rep"),
        P("rep", exp),
        P(exp, None, "rep"),
        P(exp, None, "rep"),
        P(exp, "rep", None),
        P(exp, "rep"),
        P(exp, None),
        P(exp, None),
    )
    return jax.shard_map(
        on_device, mesh=fine, in_specs=in_specs, out_specs=P(exp, "rep"), check_vma=False
    )
```

```python
import functools

import jax
import jax.numpy as jnp
from jax import lax
from jax.experimental import pallas as pl
from jax.experimental.pallas import tpu as pltpu
from jax.sharding import Mesh, PartitionSpec as P


def spread(x, axis):
    copies = jnp.broadcast_to(x[None], (lax.axis_size(axis),) + x.shape)
    return lax.all_to_all(copies, axis, split_axis=0, concat_axis=0, tiled=True)


def expert_counts(ids_t, experts):
    tok = ids_t.shape[1]
    expert = lax.broadcasted_iota(jnp.int32, (experts, tok), 0)
    one_hot = jnp.zeros((experts, tok), jnp.bool_)
    for k in range(ids_t.shape[0]):
        one_hot = one_hot | (ids_t[k][None, :] == expert)
    earlier = lax.broadcasted_iota(jnp.int32, (tok, tok), 0) < lax.broadcasted_iota(
        jnp.int32, (tok, tok), 1
    )
    counts = jnp.dot(
        one_hot.astype(jnp.bfloat16),
        earlier.astype(jnp.bfloat16),
        preferred_element_type=jnp.float32,
    ).astype(jnp.int32)
    return one_hot, counts


def expert_kernel(x_ref, w_ref, out_ref, y_ref):
    hid = out_ref.shape[0]
    act = jnp.dot(x_ref[...], w_ref[...], preferred_element_type=jnp.float32)
    hidden = (jax.nn.silu(act[:, :hid]) * act[:, hid:]).astype(jnp.bfloat16)
    chunk = min(512, y_ref.shape[1])
    for c in range(0, y_ref.shape[1], chunk):
        y_ref[:, c : c + chunk] = jnp.dot(
            hidden, out_ref[:, c : c + chunk], preferred_element_type=jnp.float32
        ).astype(jnp.bfloat16)


def run_expert(x, w, out, parts=2):
    rows, width = x.shape
    hid = out.shape[0]
    block = rows // parts
    return pl.pallas_call(
        expert_kernel,
        grid=(parts,),
        in_specs=[
            pl.BlockSpec((block, width), lambda i: (i, 0)),
            pl.BlockSpec((width, 2 * hid), lambda i: (0, 0)),
            pl.BlockSpec((hid, width), lambda i: (0, 0)),
        ],
        out_specs=pl.BlockSpec((block, width), lambda i: (i, 0)),
        out_shape=jax.ShapeDtypeStruct((rows, width), jnp.bfloat16),
        compiler_params=pltpu.CompilerParams(vmem_limit_bytes=56 * 1024 * 1024),
        cost_estimate=pl.CostEstimate(
            flops=6 * rows * width * hid,
            bytes_accessed=2 * (2 * rows * width + 3 * width * hid),
            transcendentals=rows * hid,
        ),
    )(x, w, out)


def mix_kernel(per, x_ref, w_ref, o_ref, total):
    step = pl.program_id(0)

    @pl.when(step == 0)
    def _():
        total[...] = jnp.zeros_like(total)

    for j in range(per):
        toks, depth = total.shape[0], 2 * x_ref.shape[2]
        x = jnp.concatenate([x_ref[j, :toks], x_ref[j, toks:]], axis=1)
        w = w_ref[:, j].reshape(depth, w_ref.shape[3])
        total[...] += jnp.dot(x, w, preferred_element_type=jnp.float32)

    @pl.when(step == pl.num_programs(0) - 1)
    def _():
        o_ref[...] = total[...].astype(jnp.bfloat16)


def run_mix(x, w, per=4):
    ny, toks, depth = x.shape[0], x.shape[1] // 2, 2 * x.shape[2]
    nk, _, unit, cols = w.shape
    return pl.pallas_call(
        functools.partial(mix_kernel, per),
        grid=(ny // per,),
        in_specs=[
            pl.BlockSpec((per, 2 * toks, depth // 2), lambda i: (i, 0, 0)),
            pl.BlockSpec((nk, per, unit, cols), lambda i: (0, i, 0, 0)),
        ],
        out_specs=pl.BlockSpec((toks, cols), lambda i: (0, 0)),
        out_shape=jax.ShapeDtypeStruct((toks, cols), jnp.bfloat16),
        scratch_shapes=[pltpu.VMEM((toks, cols), jnp.float32)],
        compiler_params=pltpu.CompilerParams(vmem_limit_bytes=56 * 1024 * 1024),
        cost_estimate=pl.CostEstimate(
            flops=2 * ny * toks * depth * cols,
            bytes_accessed=2 * ny * depth * cols,
            transcendentals=0,
        ),
    )(x, w)


def slot_mask(one_hot, counts, capacity):
    experts, toks = counts.shape
    shape = (experts, 2 * capacity, 2 * toks)
    row = lax.broadcasted_iota(jnp.int32, shape, 1)
    col = lax.broadcasted_iota(jnp.int32, shape, 2)
    row_half = (row >= capacity).astype(jnp.int32)
    col_half = (col >= toks).astype(jnp.int32)
    slot = jnp.where(one_hot, counts, -1)
    slot = jnp.concatenate([slot, slot], axis=1)[:, None, :]
    return (slot == row - capacity * row_half) & (row_half == col_half)


def combine_weights(ids_t, gates_t, experts, capacity):
    one_hot, counts = expert_counts(ids_t, experts)
    expert = lax.broadcasted_iota(jnp.int32, counts.shape, 0)
    gate = jnp.zeros(counts.shape, jnp.float32)
    for k in range(ids_t.shape[0]):
        gate = gate + jnp.where(ids_t[k][None, :] == expert, gates_t[k][None, :], 0.0)
    high = lax.reduce_precision(gate, 8, 7)
    mask = slot_mask(one_hot, counts, capacity)

    def spread_out(g):
        both = jnp.concatenate([g, g], axis=1)[:, None, :]
        return jnp.where(mask, both, 0.0).astype(jnp.bfloat16).reshape(-1, mask.shape[2])

    return spread_out(high), spread_out(gate - high)


def on_device(
    tokens, down_weight, gate_proj, up_proj, out_proj, up_weight, expert_ids, route_gates
):
    tok_rows = tokens.shape[0]
    topk_count = expert_ids.shape[1]
    ny, nk, nr = lax.axis_size("y"), lax.axis_size("k"), lax.axis_size("rep")
    experts = ny * nk
    capacity = max(2, 3 * tok_rows * topk_count // (2 * experts))
    width = gate_proj.shape[1]
    unit = down_weight.shape[1]
    slice_width = width // nr

    swap = [(i * nr + j, j * nr + i) for i in range(nk) for j in range(nr)]
    copies = jnp.broadcast_to(down_weight.T[None], (ny, unit, down_weight.shape[0]))
    ids_t = expert_ids.T
    after, copies = lax.optimization_barrier((ids_t, copies))
    sent_ids_t = lax.ppermute(after, ("k", "rep"), swap)

    all_tokens = lax.all_gather(tokens, "k", axis=0, tiled=True)
    down_cols = lax.all_to_all(copies, "y", split_axis=0, concat_axis=0, tiled=True).reshape(ny * unit, down_weight.shape[0])
    one_hot, counts = expert_counts(sent_ids_t, experts)
    select = slot_mask(one_hot, counts, capacity).astype(jnp.bfloat16)
    select = select.reshape(2 * experts * capacity, 2 * tok_rows)

    partial_latent = lax.dot_general(
        all_tokens, down_cols, (((1,), (1,)), ((), ())), preferred_element_type=jnp.float32
    )
    partial_latent, select = lax.optimization_barrier(
        (partial_latent.astype(jnp.bfloat16), select)
    )
    pieces = lax.all_to_all(
        partial_latent.reshape(nr, tok_rows, ny * unit),
        "rep", split_axis=0, concat_axis=0, tiled=True,
    )
    latent = jnp.sum(pieces.astype(jnp.float32), axis=0).astype(jnp.bfloat16)
    half = ny * unit // 2
    latent = jnp.concatenate([latent[:, :half], latent[:, half:]], axis=0)
    send = jnp.dot(select, latent, preferred_element_type=jnp.float32).astype(jnp.bfloat16)
    got = lax.all_to_all(
        send.reshape(experts, 2 * capacity, half),
        ("y", "k"), split_axis=0, concat_axis=0, tiled=True,
    )
    rows = got.reshape(ny, nk, 2, capacity, half).transpose(3, 0, 1, 2, 4)
    rows = rows.reshape(capacity * ny, width)
    rows, up_weight = lax.optimization_barrier((rows, up_weight))
    full_rows = lax.all_gather(rows, "rep", axis=0, tiled=True)
    up_rows = spread(up_weight, "y")

    def reorder(w):
        return w.reshape(ny, nk, unit, w.shape[1]).transpose(1, 0, 2, 3).reshape(w.shape)

    high, low = combine_weights(expert_ids.T, route_gates.T, experts, capacity)
    weights = jnp.concatenate([reorder(gate_proj[0]), reorder(up_proj[0])], axis=1)
    full_rows, weights, high, low, up_rows = lax.optimization_barrier(
        (full_rows, weights, high, low, up_rows)
    )
    partial_out = run_expert(full_rows, weights, out_proj[0])
    finished = lax.psum_scatter(partial_out, "rep", scatter_dimension=1, tiled=True)
    finished, up_rows = lax.optimization_barrier((finished, up_rows))
    all_up = lax.all_gather(up_rows, "k", axis=0, tiled=False)
    back = finished.reshape(nr, capacity, ny, 2, slice_width // 2).transpose(2, 0, 3, 1, 4)
    returned = lax.all_to_all(
        back.reshape(experts, 2 * capacity, slice_width // 2),
        ("y", "k"), split_axis=0, concat_axis=0, tiled=True,
    )
    returned = returned.reshape(2 * experts * capacity, slice_width // 2)
    combined = sum(
        lax.dot_general(
            g, returned, (((0,), (0,)), ((), ())), preferred_element_type=jnp.float32
        )
        for g in (high, low)
    ).astype(jnp.bfloat16)
    return run_mix(spread(combined, "rep"), all_up)


def solution(mesh):
    nexp, nrep = mesh.devices.shape
    fine = Mesh(mesh.devices.reshape(nexp // nrep, nrep, nrep), ("y", "k", "rep"))
    exp = ("y", "k")
    in_specs = (
        P(exp, "rep"),
        P("rep", exp),
        P(exp, None, "rep"),
        P(exp, None, "rep"),
        P(exp, "rep", None),
        P(exp, "rep"),
        P(exp, None),
        P(exp, None),
    )
    return jax.shard_map(
        on_device, mesh=fine, in_specs=in_specs, out_specs=P(exp, "rep"), check_vma=False
    )
```
